128 devices in a mesh: expert: 16 (over y, z), dp: 8 (over x, core).
Axes of the slice: x: 4, y: 4, z: 4, core: 2. Of those that a mesh axis runs over, the one named last changes fastest.
Arguments:
- grad_parts: bfloat16 [8, 16, 3584, 1024], P('dp', 'expert'), may hold values from -6 to 6
- owner_slot: int32 [16], replicated, may hold values from 0 to 15, each once
- slot_expert: int32 [16, 2], replicated, may hold values from 0 to 15, all different within a row
- master: float32 [16, 3584, 1024], P(None, 'expert', 'dp'), may hold values from -1.5 to 1.5
- moment_one: float32 [16, 3584, 1024], P(None, 'expert', 'dp'), may hold values from -2 to 2
- moment_two: float32 [16, 3584, 1024], P(None, 'expert', 'dp'), may hold values from 0.01 to 1
- ema_weights: float32 [16, 3584, 1024], P(None, 'expert', 'dp'), may hold values from -1.5 to 1.5
Outputs:
- master_out: float32 [16, 3584, 1024], P(None, 'expert', 'dp')
- moment_one_out: float32 [16, 3584, 1024], P(None, 'expert', 'dp')
- moment_two_out: float32 [16, 3584, 1024], P(None, 'expert', 'dp')
- ema_out: float32 [16, 3584, 1024], P(None, 'expert', 'dp')
- replicas: bfloat16 [32, 3584, 1024], P('expert', None, 'dp')
The draws below stay inside these ranges and needn't reach their ends.
Inputs may be any that keep to these rules, and one draw needn't show every extreme that they name: `owner_slot`: a permutation of the 16 experts; position k belongs to expert-axis index k. `slot_expert`: each row names 2 different experts, and every expert is named by some row.
All inputs are finite; a program needn't handle non-finite values.
Results may differ from the reference program's by a relative error of at most 0.009.
Values may be sent and summed in bfloat16 or wider, within the bound.
No kernel may reach another device: no remote copies, remote signals or barrier semaphores. Data moves between devices by JAX's collectives and lax.ppermute only.
A program may use at most 128 MiB of HBM per device.

```python
import math
import jax
import jax.numpy as jnp
from jax import lax

ROWS = 3584
HIDDEN_SIZE = 1024
SLOTS = 2
STEP = 10
EXPERTS = 16
N_EXPERT = 16
N_DP = 8


def spiked(result, own_key, source, target, parts, factor):
    def block_of(axis_at):
        return (jnp.arange(result.shape[axis_at]) // (result.shape[axis_at] // parts)).reshape((-1,) + (1,) * (result.ndim - 1 - axis_at))

    near = jax.random.permutation(own_key, parts)[block_of(target)]
    second = (block_of(target) + parts // 2) % parts
    return jnp.where((block_of(source) == near) | (block_of(source) == second), factor * result, result)


def shard_levels(rng, dims, pieces, least, high):
    def one(position, shards_of):
        heights = jax.random.uniform(jax.random.fold_in(jax.random.fold_in(rng, 6), position), (shards_of,), jnp.float32, least / len(pieces), high / len(pieces))
        return jnp.repeat(jnp.exp(heights), dims[position] // shards_of).reshape((-1,) + (1,) * (len(dims) - position - 1))

    factor_of = one(*pieces[0])
    for cut in pieces[1:]:
        factor_of = factor_of * one(*cut)
    return factor_of


def choose_distinct(rng, rows, count, top, lift):
    ranking = jax.random.permutation(jax.random.fold_in(rng, 1), count)
    pull = ranking
    for power in range(3):
        pull = pull * pull // count
    pull = pull * lift // count
    tickets = jax.random.randint(jax.random.fold_in(rng, 2), (rows, count), 0, 4096) + pull
    fixed_rows = jax.random.permutation(jax.random.fold_in(rng, 3), rows)[jnp.arange(count) % rows]
    tickets = jnp.where(jnp.arange(rows)[:, None] == fixed_rows[None, :], 1 << 14, tickets)
    priority = tickets * count + jnp.arange(count)
    return lax.top_k(priority.astype(jnp.int32), top)[1].astype(jnp.int32)


def noise(stream_key, dims, scale, most, split=(), kind=jnp.bfloat16):
    drawn = jax.random.normal(stream_key, dims, jnp.float32) * scale
    if len(split) > 0:
        drawn = shard_levels(stream_key, dims, split, -0.22, 0.18) * drawn
    return jnp.clip(drawn, min=-most, max=most).astype(kind)


def gaussian_with(own_key, shape, width, limit, split, heavy, kind=jnp.bfloat16):
    result = width * jax.random.normal(own_key, shape, jnp.float32)
    if split:
        result = result * shard_levels(own_key, shape, split, -0.22, 0.18)
    return jnp.clip(spiked(result, jax.random.fold_in(own_key, 3), *heavy), -limit, limit).astype(kind)


def setup_inputs(seed: int = 0) -> dict:
    seeds = jax.random.split(jax.random.key(seed), 8)
    grad_parts = gaussian_with(seeds[0], (N_DP, EXPERTS, ROWS, HIDDEN_SIZE), 1.0, 6.0, ((0, 8), (1, 16)), (0, 3, 8, 2.0))
    owner_slot = jax.random.permutation(seeds[1], EXPERTS).astype(jnp.int32)
    slot_expert = choose_distinct(seeds[2], N_EXPERT, EXPERTS, SLOTS, 2048)
    master = noise(seeds[3], (EXPERTS, ROWS, HIDDEN_SIZE), 0.25, 1.5, ((1, 16), (2, 8)), jnp.float32)
    moment_one = noise(seeds[4], (EXPERTS, ROWS, HIDDEN_SIZE), 0.3, 2.0, ((1, 16), (2, 8)), jnp.float32)
    moment_two = jnp.clip(jnp.exp(math.log(1.0) - 4.6051702 * jax.random.uniform(seeds[5], (EXPERTS, ROWS, HIDDEN_SIZE), jnp.float32) ** shard_levels(seeds[5], (EXPERTS, ROWS, HIDDEN_SIZE), ((1, 16), (2, 8)), -0.2, 0.2)), 0.01, 1.0)
    ema_weights = noise(seeds[6], (EXPERTS, ROWS, HIDDEN_SIZE), 0.25, 1.5, ((1, 16), (2, 8)), jnp.float32)
    return {"grad_parts": grad_parts, "owner_slot": owner_slot, "slot_expert": slot_expert, "master": master, "moment_one": moment_one, "moment_two": moment_two, "ema_weights": ema_weights}


beta_one = 0.9
beta_two = 0.999
adam_eps = 1e-08
learn_rate = 0.05
decay_rate = 0.1
ema_decay = 0.99

def reference(grad_parts, owner_slot, slot_expert, master, moment_one, moment_two, ema_weights):
    summed = grad_parts[0].astype(jnp.float32)
    for copy_index in range(1, N_DP):
        summed = summed + grad_parts[copy_index].astype(jnp.float32)
    gradient = jnp.take(summed, owner_slot, axis=0)
    correct_one = 1.0 - beta_one ** STEP
    correct_two = 1.0 - beta_two ** STEP
    moment_one_out = beta_one * moment_one + (1.0 - beta_one) * gradient
    moment_two_out = beta_two * moment_two + (1.0 - beta_two) * gradient * gradient
    update = moment_one_out / correct_one / (jnp.sqrt(moment_two_out / correct_two) + adam_eps)
    master_out = master - learn_rate * (update + decay_rate * master)
    ema_out = ema_decay * ema_weights + (1.0 - ema_decay) * master_out
    replicas = jnp.take(master_out, slot_expert.reshape(-1), axis=0).astype(jnp.bfloat16)
    return (master_out, moment_one_out, moment_two_out, ema_out, replicas)
```

```python
import jax
import jax.numpy as jnp
from jax import lax
from jax.experimental import pallas as pl
from jax.experimental.pallas import tpu as pltpu
from jax.sharding import PartitionSpec as P

STEP = 10

beta_one = 0.9
beta_two = 0.999
adam_eps = 1e-08
learn_rate = 0.05
decay_rate = 0.1
ema_decay = 0.99

F32 = jnp.float32
BF16 = jnp.bfloat16
LANES = 128
CHUNKS = (912, 880)
LIMIT = 48 * 1024 * 1024
ANY = pl.BlockSpec(memory_space=pl.ANY)


def params():
    return pltpu.CompilerParams(vmem_limit_bytes=LIMIT)


def column(place_ref, x, core):
    return pl.ds(pl.multiple_of((2 * x + core) * LANES, LANES), LANES)


def for_partner(grad, place):
    def kernel(place_ref, grad_ref, *rest):
        sems = rest[-1]
        copies = []
        start = 0
        for chunk, half in enumerate(CHUNKS):
            for x in range(4):
                copies.append(
                    pltpu.make_async_copy(
                        grad_ref.at[pl.ds(start, 2 * half), column(place_ref, x, 1 - place_ref[1])],
                        rest[chunk].at[x],
                        sems.at[chunk, x],
                    )
                )
            start += 2 * half
        for copy in copies:
            copy.start()
        for copy in copies:
            copy.wait()

    return pl.pallas_call(
        kernel,
        out_shape=[jax.ShapeDtypeStruct((4, 2 * half, LANES), BF16) for half in CHUNKS],
        in_specs=[pl.BlockSpec(memory_space=pltpu.SMEM), ANY],
        out_specs=[ANY] * len(CHUNKS),
        scratch_shapes=[pltpu.SemaphoreType.DMA((len(CHUNKS), 4))],
        compiler_params=params(),
        name="for_partner",
    )(place, grad)


def add_up(name, place, grad, near, start, half, terms, outs, others, before=None):
    n_others = len(others)
    n_in = 2 + max(len(term[2]) for term in terms)

    def kernel(place_ref, grad_ref, near_ref, *rest):
        other_refs = rest[:n_others]
        rest = rest[n_others + (before is not None) :]
        out_refs = rest[: len(outs)]
        held, total, in_sems, out_sems = rest[len(outs) :]
        coming, going = [], []
        for t, (h, mask, received, (out, at)) in enumerate(terms):
            x = place_ref[0] ^ mask
            sources = [
                grad_ref.at[pl.ds(start + h * half, half), column(place_ref, x, place_ref[1])],
                near_ref.at[x, pl.ds(h * half, half)],
            ] + [other_refs[o].at[i] if i else other_refs[o] for o, i in received]
            coming.append(
                [
                    pltpu.make_async_copy(source, held.at[t, k], in_sems.at[t, k])
                    for k, source in enumerate(sources)
                ]
            )
            going.append(pltpu.make_async_copy(total.at[t], out_refs[out].at[at] if at else out_refs[out], out_sems.at[t]))
        for copies in coming:
            for copy in copies:
                copy.start()
        for t, copies in enumerate(coming):
            for copy in copies:
                copy.wait()
            value = held[t, 0].astype(F32)
            for k in range(1, len(copies)):
                value = value + held[t, k].astype(F32)
            total[t] = value.astype(BF16)
            going[t].start()
        for copy in going:
            copy.wait()

    operands = (place, grad, near, *others) + (() if before is None else (before,))
    return pl.pallas_call(
        kernel,
        out_shape=[jax.ShapeDtypeStruct(out, BF16) for out in outs],
        in_specs=[pl.BlockSpec(memory_space=pltpu.SMEM)] + [ANY] * (len(operands) - 1),
        out_specs=[ANY] * len(outs),
        scratch_shapes=[
            pltpu.VMEM((len(terms), n_in, half, LANES), BF16),
            pltpu.VMEM((len(terms), half, LANES), BF16),
            pltpu.SemaphoreType.DMA((len(terms), n_in)),
            pltpu.SemaphoreType.DMA((len(terms),)),
        ],
        input_output_aliases={} if before is None else {len(operands) - 1: 0},
        compiler_params=params(),
        name=name,
    )(*operands)


def first_terms(place, grad, near, start, half):
    terms = [(h, mask, (), (h, (j,))) for h in (0, 1) for j, mask in enumerate((1 + 2 * h, 2))]
    return add_up("first_terms", place, grad, near, start, half, terms, [(2, half, LANES)] * 2, ())


def second_terms(place, grad, near, got, start, half):
    terms = [(h, 3 - 2 * h, ((h, (1,)),), (h, ())) for h in (0, 1)]
    return add_up("second_terms", place, grad, near, start, half, terms, [(half, LANES)] * 2, got)


def all_terms(place, grad, near, got, last, start, half, before):
    terms = [
        (h, 0, ((h, (0,)), (2 + h, ())), (0, (pl.ds(start + h * half, half),))) for h in (0, 1)
    ]
    outs = [(grad.shape[0], LANES)]
    return add_up("all_terms", place, grad, near, start, half, terms, outs, (*got, *last), before)[0]


def adam(gradient, master, moment_one, moment_two):
    correct_one = 1.0 - beta_one**STEP
    correct_two = 1.0 - beta_two**STEP
    one = beta_one * moment_one + (1.0 - beta_one) * gradient
    two = beta_two * moment_two + (1.0 - beta_two) * gradient * gradient
    update = one / (jnp.sqrt(two * (1.0 / correct_two)) + adam_eps)
    return (1.0 - learn_rate * decay_rate) * master - (learn_rate / correct_one) * update, one, two


GROUP = 4


def replica_terms(rows, owner_slot, slot_expert, master, moment_one, moment_two):
    experts, height, lanes = master.shape
    hosts, slots = slot_expert.shape

    def kernel(owner_ref, slot_ref, rows_ref, master_ref, one_ref, two_ref, out_ref, updated):
        step = pl.program_id(0)
        for k in range(GROUP):
            e = step * GROUP + k
            gradient = rows_ref[owner_ref[e]].astype(F32)
            updated[e] = adam(gradient, master_ref[k], one_ref[k], two_ref[k])[0].astype(BF16)

        @pl.when(step == experts // GROUP - 1)
        def _():
            for g in range(hosts):
                for s in range(slots):
                    out_ref[g, s] = updated[slot_ref[g, s]]

    state = pl.BlockSpec((GROUP, height, lanes), lambda i, *_: (i, 0, 0))
    return pl.pallas_call(
        kernel,
        out_shape=pltpu.HBM((hosts, slots, height, lanes), BF16),
        grid_spec=pltpu.PrefetchScalarGridSpec(
            num_scalar_prefetch=2,
            grid=(experts // GROUP,),
            in_specs=[pl.BlockSpec(rows.shape, lambda i, *_: (0, 0, 0)), state, state, state],
            out_specs=pl.BlockSpec((hosts, slots, height, lanes), lambda i, *_: (0, 0, 0, 0)),
            scratch_shapes=[pltpu.VMEM((experts, height, lanes), BF16)],
        ),
        compiler_params=params(),
        name="replica_terms",
    )(owner_slot, slot_expert, rows, master, moment_one, moment_two)


def new_state(rows, owner_slot, master, moment_one, moment_two, ema_weights):
    experts, height, lanes = master.shape

    def kernel(owner_ref, rows_ref, master_ref, one_ref, two_ref, ema_ref, master_out, one_out, two_out, ema_out):
        for k in range(GROUP):
            gradient = rows_ref[owner_ref[pl.program_id(0) * GROUP + k]].astype(F32)
            weights, one, two = adam(gradient, master_ref[k], one_ref[k], two_ref[k])
            master_out[k] = weights
            one_out[k] = one
            two_out[k] = two
            ema_out[k] = ema_decay * ema_ref[k] + (1.0 - ema_decay) * weights

    state = pl.BlockSpec((GROUP, height, lanes), lambda i, *_: (i, 0, 0))
    return pl.pallas_call(
        kernel,
        out_shape=[jax.ShapeDtypeStruct(master.shape, F32)] * 4,
        grid_spec=pltpu.PrefetchScalarGridSpec(
            num_scalar_prefetch=1,
            grid=(experts // GROUP,),
            in_specs=[pl.BlockSpec(rows.shape, lambda i, *_: (0, 0, 0)), state, state, state, state],
            out_specs=[state] * 4,
        ),
        compiler_params=params(),
        name="new_state",
    )(owner_slot, rows, master, moment_one, moment_two, ema_weights)


def by_slot(blocks):
    sources, slots, height, lanes = blocks.shape

    def kernel(in_ref, out_ref, sems):
        copies = [pltpu.make_async_copy(in_ref.at[:, s], out_ref.at[s], sems.at[s]) for s in range(slots)]
        for copy in copies:
            copy.start()
        for copy in copies:
            copy.wait()

    return pl.pallas_call(
        kernel,
        out_shape=jax.ShapeDtypeStruct((slots, sources, height, lanes), BF16),
        in_specs=[pl.BlockSpec(memory_space=pl.ANY)],
        out_specs=pl.BlockSpec(memory_space=pl.ANY),
        scratch_shapes=[pltpu.SemaphoreType.DMA((slots,))],
        compiler_params=params(),
        name="by_slot",
    )(blocks)


def exchange(value, mask):
    return lax.ppermute(value, "dp", [(i, i ^ mask) for i in range(8)])


def after(value, other):
    return lax.optimization_barrier((value, other))[0]


def per_device(grad_parts, owner_slot, slot_expert, master, moment_one, moment_two, ema_weights):
    grad = grad_parts[0, 0]
    total_rows = grad.shape[0]
    experts, height, _ = master.shape
    me = lax.axis_index("dp").astype(jnp.int32)
    place = jnp.stack([me // 2, me % 2])

    starts = [2 * sum(CHUNKS[:k]) for k in range(len(CHUNKS))]
    nears = [exchange(block, 1) for block in for_partner(grad, place)]
    gots, lasts = [], []
    for start, half, near in zip(starts, CHUNKS, nears):
        a, b = first_terms(place, grad, near, start, half)
        gots.append((exchange(a, 2), exchange(b, 6)))
        place = after(place, a)
    for start, half, near, got in zip(starts, CHUNKS, nears, gots):
        a, b = second_terms(place, grad, near, got, start, half)
        lasts.append((exchange(a, 6), exchange(b, 2)))
        place = after(place, a)
    summed = None
    for start, half, near, got, last in zip(starts, CHUNKS, nears, gots, lasts):
        summed = all_terms(place, grad, near, got, last, start, half, summed)

    rows = lax.all_to_all(
        summed.reshape(experts, height, LANES), "expert", split_axis=0, concat_axis=0, tiled=True
    )
    to_hosts = replica_terms(rows, owner_slot, slot_expert, master, moment_one, moment_two)
    state = new_state(rows, owner_slot, master, moment_one, moment_two, ema_weights)
    replicas = lax.all_to_all(to_hosts, "expert", split_axis=0, concat_axis=0, tiled=True)
    replicas = by_slot(replicas).reshape(-1, total_rows, LANES)
    return (*state, replicas)


def solution(mesh):
    placed = (
        P("dp", "expert", None, None),
        P(),
        P(),
        P(None, "expert", "dp"),
        P(None, "expert", "dp"),
        P(None, "expert", "dp"),
        P(None, "expert", "dp"),
    )
    return jax.shard_map(
        per_device,
        mesh=mesh,
        in_specs=placed,
        out_specs=(
            P(None, "expert", "dp"),
            P(None, "expert", "dp"),
            P(None, "expert", "dp"),
            P(None, "expert", "dp"),
            P("expert", None, "dp"),
        ),
        check_vma=False,
    )
```

```python
import jax
import jax.numpy as jnp
from jax import lax
from jax.experimental import pallas as pl
from jax.experimental.pallas import tpu as pltpu
from jax.sharding import PartitionSpec as P

STEP = 10

beta_one = 0.9
beta_two = 0.999
adam_eps = 1e-08
learn_rate = 0.05
decay_rate = 0.1
ema_decay = 0.99

F32 = jnp.float32
BF16 = jnp.bfloat16
LANES = 128
CHUNKS = (448, 800, 544)
FLOPS = {"for_partner": 10000000000, "first_terms": 10000000000, "second_terms": 1000000000, "all_terms": 1000000000}
LIMIT = 32 * 1024 * 1024
ANY = pl.BlockSpec(memory_space=pl.ANY)


def params(limit=LIMIT):
    return pltpu.CompilerParams(vmem_limit_bytes=limit)


def column(place_ref, x, core):
    return pl.ds(pl.multiple_of((2 * x + core) * LANES, LANES), LANES)


def for_partner(place, grad, start, halves):
    def kernel(place_ref, grad_ref, *rest):
        sems = rest[-1]
        copies = []
        at = start
        for chunk, half in enumerate(halves):
            for x in range(4):
                copies.append(
                    pltpu.make_async_copy(
                        grad_ref.at[pl.ds(at, 2 * half), column(place_ref, x, 1 - place_ref[1])],
                        rest[chunk].at[x],
                        sems.at[chunk, x],
                    )
                )
            at += 2 * half
        for copy in copies:
            copy.start()
        for copy in copies:
            copy.wait()

    return pl.pallas_call(
        kernel,
        out_shape=[jax.ShapeDtypeStruct((4, 2 * half, LANES), BF16) for half in halves],
        in_specs=[pl.BlockSpec(memory_space=pltpu.SMEM), ANY],
        out_specs=[ANY] * len(halves),
        scratch_shapes=[pltpu.SemaphoreType.DMA((len(halves), 4))],
        compiler_params=params(),
        cost_estimate=pl.CostEstimate(flops=FLOPS["for_partner"], bytes_accessed=1000, transcendentals=0),
        name="for_partner",
    )(place, grad)


def whole(shape):
    return pl.BlockSpec(shape, lambda i: (0,) * len(shape))


def add_up(name, place, arrays, terms, outs, in_place=True, before=None):
    most = max(term[0] for term in terms)
    n_arrays = len(arrays)

    def kernel(place_ref, *rest):
        refs = rest[:n_arrays]
        rest = rest[n_arrays + (before is not None) :]
        out_refs = rest[: len(outs)]
        held, in_sems = rest[len(outs) : len(outs) + 2]
        coming, going = [], []
        for t, (rows, sources, (out, at)) in enumerate(terms):
            part = pl.ds(0, rows)
            index = sources[0][1]
            coming.append(
                pltpu.make_async_copy(refs[0].at[index(place_ref)], held.at[t, part], in_sems.at[t])
            )
            coming[-1].start()
            if not in_place:
                total, out_sems = rest[len(outs) + 2 :]
                going.append(pltpu.make_async_copy(total.at[t, part], out_refs[out].at[at], out_sems.at[t]))
        for t, (rows, sources, (out, at)) in enumerate(terms):
            coming[t].wait()
            value = held[t, pl.ds(0, rows)].astype(F32)
            for array, index in sources[1:]:
                value = value + refs[array][index(place_ref)].astype(F32)
            if in_place:
                out_refs[out][at] = value.astype(BF16)
            else:
                total[t, pl.ds(0, rows)] = value.astype(BF16)
                going[t].start()
        for copy in going:
            copy.wait()

    operands = (place, *arrays) + (() if before is None else (before,))
    scratch = [pltpu.VMEM((len(terms), most, LANES), BF16), pltpu.SemaphoreType.DMA((len(terms),))]
    return pl.pallas_call(
        kernel,
        grid=(1,),
        out_shape=[jax.ShapeDtypeStruct(out, BF16) for out in outs],
        in_specs=[pl.BlockSpec(memory_space=pltpu.SMEM), ANY]
        + [whole(array.shape) for array in arrays[1:]]
        + [ANY] * (before is not None),
        out_specs=[whole(out) if in_place else ANY for out in outs],
        scratch_shapes=scratch * (1 if in_place else 2),
        input_output_aliases={} if before is None else {len(operands) - 1: 0},
        compiler_params=params(),
        cost_estimate=pl.CostEstimate(flops=FLOPS[name], bytes_accessed=1000, transcendentals=0),
        name=name,
    )(*operands)


def own(start, half, h, mask):
    rows = pl.ds(start + h * half, half)
    return (0, lambda place_ref: (rows, column(place_ref, place_ref[0] ^ mask, place_ref[1])))


def partner(array, half, h, mask):
    rows = pl.ds(h * half, half)
    return (array, lambda place_ref: (place_ref[0] ^ mask, rows))


def first_terms(place, grad, near, start, half):
    terms = [
        (half, [own(start, half, h, mask), partner(1, half, h, mask)], (h, (j,)))
        for h in (0, 1)
        for j, mask in enumerate((1 + 2 * h, 2))
    ]
    return add_up("first_terms", place, (grad, near), terms, [(2, half, LANES)] * 2)


def second_terms(place, grad, near, got, start, half):
    terms = [
        (half, [own(start, half, h, 3 - 2 * h), partner(1, half, h, 3 - 2 * h), (2 + h, lambda _: (1,))], (h, (slice(None),)))
        for h in (0, 1)
    ]
    return add_up("second_terms", place, (grad, near, *got), terms, [(half, LANES)] * 2)


def all_terms(place, grad, chunks, before):
    arrays, terms = [grad], []
    for start, half, near, got, last in chunks:
        base = len(arrays)
        arrays += [near, *got, *last]
        for h in (0, 1):
            sources = [
                own(start, half, h, 0),
                partner(base, half, h, 0),
                (base + 1 + h, lambda _: (0,)),
                (base + 3 + h, lambda _: (slice(None),)),
            ]
            terms.append((half, sources, (0, (pl.ds(start + h * half, half),))))
    return add_up("all_terms", place, arrays, terms, [(grad.shape[0], LANES)], False, before)[0]


def adam(gradient, master, moment_one, moment_two):
    correct_one = 1.0 - beta_one**STEP
    correct_two = 1.0 - beta_two**STEP
    one = beta_one * moment_one + (1.0 - beta_one) * gradient
    two = beta_two * moment_two + (1.0 - beta_two) * gradient * gradient
    scaled = two * (1.0 / correct_two)
    update = one / (scaled * lax.rsqrt(scaled) + adam_eps)
    return (1.0 - learn_rate * decay_rate) * master - (learn_rate / correct_one) * update, one, two


GROUP = 8
STATE_GROUP = 4


def replica_terms(rows, owner_slot, slot_expert, master, moment_one, moment_two):
    experts, height, lanes = master.shape
    hosts, slots = slot_expert.shape

    def kernel(owner_ref, slot_ref, rows_ref, master_ref, one_ref, two_ref, out_ref, updated):
        step = pl.program_id(0)
        for k in range(GROUP):
            e = step * GROUP + k
            gradient = rows_ref[owner_ref[e]].astype(F32)
            updated[e] = adam(gradient, master_ref[k], one_ref[k], two_ref[k])[0].astype(BF16)

        @pl.when(step == experts // GROUP - 1)
        def _():
            for g in range(hosts):
                for s in range(slots):
                    out_ref[g, s] = updated[slot_ref[g, s]]

    state = pl.BlockSpec((GROUP, height, lanes), lambda i, *_: (i, 0, 0))
    return pl.pallas_call(
        kernel,
        out_shape=pltpu.HBM((hosts, slots, height, lanes), BF16),
        grid_spec=pltpu.PrefetchScalarGridSpec(
            num_scalar_prefetch=2,
            grid=(experts // GROUP,),
            in_specs=[pl.BlockSpec(rows.shape, lambda i, *_: (0, 0, 0)), state, state, state],
            out_specs=pl.BlockSpec((hosts, slots, height, lanes), lambda i, *_: (0, 0, 0, 0)),
            scratch_shapes=[pltpu.VMEM((experts, height, lanes), BF16)],
        ),
        compiler_params=params(48 * 1024 * 1024),
        name="replica_terms",
    )(owner_slot, slot_expert, rows, master, moment_one, moment_two)


def new_state(rows, owner_slot, master, moment_one, moment_two, ema_weights):
    experts, height, lanes = master.shape

    def kernel(owner_ref, rows_ref, master_ref, one_ref, two_ref, ema_ref, master_out, one_out, two_out, ema_out):
        for k in range(STATE_GROUP):
            gradient = rows_ref[owner_ref[pl.program_id(0) * STATE_GROUP + k]].astype(F32)
            weights, one, two = adam(gradient, master_ref[k], one_ref[k], two_ref[k])
            master_out[k] = weights
            one_out[k] = one
            two_out[k] = two
            ema_out[k] = ema_decay * ema_ref[k] + (1.0 - ema_decay) * weights

    state = pl.BlockSpec((STATE_GROUP, height, lanes), lambda i, *_: (i, 0, 0))
    return pl.pallas_call(
        kernel,
        out_shape=[jax.ShapeDtypeStruct(master.shape, F32)] * 4,
        grid_spec=pltpu.PrefetchScalarGridSpec(
            num_scalar_prefetch=1,
            grid=(experts // STATE_GROUP,),
            in_specs=[pl.BlockSpec(rows.shape, lambda i, *_: (0, 0, 0)), state, state, state, state],
            out_specs=[state] * 4,
        ),
        compiler_params=params(48 * 1024 * 1024),
        name="new_state",
    )(owner_slot, rows, master, moment_one, moment_two, ema_weights)


def by_slot(blocks):
    sources, slots, height, lanes = blocks.shape

    def kernel(in_ref, out_ref, sems):
        copies = [pltpu.make_async_copy(in_ref.at[:, s], out_ref.at[s], sems.at[s]) for s in range(slots)]
        for copy in copies:
            copy.start()
        for copy in copies:
            copy.wait()

    return pl.pallas_call(
        kernel,
        out_shape=jax.ShapeDtypeStruct((slots, sources, height, lanes), BF16),
        in_specs=[pl.BlockSpec(memory_space=pl.ANY)],
        out_specs=pl.BlockSpec(memory_space=pl.ANY),
        scratch_shapes=[pltpu.SemaphoreType.DMA((slots,))],
        compiler_params=params(),
        name="by_slot",
    )(blocks)


def exchange(value, mask):
    return lax.ppermute(value, "dp", [(i, i ^ mask) for i in range(8)])


def after(value, other):
    return lax.optimization_barrier((value, other))[0]


def per_device(grad_parts, owner_slot, slot_expert, master, moment_one, moment_two, ema_weights):
    grad = grad_parts[0, 0]
    total_rows = grad.shape[0]
    experts, height, _ = master.shape
    me = lax.axis_index("dp").astype(jnp.int32)
    place = jnp.stack([me // 2, me % 2])

    starts = [2 * sum(CHUNKS[:k]) for k in range(len(CHUNKS))]
    first = for_partner(place, grad, 0, CHUNKS[:1])
    later = for_partner(after(place, first[0]), grad, starts[1], CHUNKS[1:])
    nears = [exchange(block, 1) for block in (*first, *later)]
    gots, lasts = [], []
    for start, half, near in zip(starts, CHUNKS, nears):
        a, b = first_terms(place, grad, near, start, half)
        gots.append((exchange(a, 2), exchange(b, 6)))
        place = after(place, a)
    for start, half, near, got in zip(starts, CHUNKS, nears, gots):
        a, b = second_terms(place, grad, near, got, start, half)
        lasts.append((exchange(a, 6), exchange(b, 2)))
        place = after(place, a)
    chunks = list(zip(starts, CHUNKS, nears, gots, lasts))
    summed = None
    for k in range(len(chunks)):
        summed = all_terms(place, grad, chunks[k : k + 1], summed)

    rows = lax.all_to_all(
        summed.reshape(experts, height, LANES), "expert", split_axis=0, concat_axis=0, tiled=True
    )
    to_hosts = replica_terms(rows, owner_slot, slot_expert, master, moment_one, moment_two)
    state = new_state(rows, owner_slot, master, moment_one, moment_two, ema_weights)
    replicas = lax.all_to_all(to_hosts, "expert", split_axis=0, concat_axis=0, tiled=True)
    replicas = by_slot(replicas).reshape(-1, total_rows, LANES)
    return (*state, replicas)


def solution(mesh):
    placed = (
        P("dp", "expert", None, None),
        P(),
        P(),
        P(None, "expert", "dp"),
        P(None, "expert", "dp"),
        P(None, "expert", "dp"),
        P(None, "expert", "dp"),
    )
    return jax.shard_map(
        per_device,
        mesh=mesh,
        in_specs=placed,
        out_specs=(
            P(None, "expert", "dp"),
            P(None, "expert", "dp"),
            P(None, "expert", "dp"),
            P(None, "expert", "dp"),
            P("expert", None, "dp"),
        ),
        check_vma=False,
    )
```

```python
import jax
import jax.numpy as jnp
from jax import lax
from jax.experimental import pallas as pl
from jax.experimental.pallas import tpu as pltpu
from jax.sharding import PartitionSpec as P

STEP = 10

beta_one = 0.9
beta_two = 0.999
adam_eps = 1e-08
learn_rate = 0.05
decay_rate = 0.1
ema_decay = 0.99

F32 = jnp.float32
BF16 = jnp.bfloat16
LANES = 128
CHUNKS = (448, 800, 544)
FLOPS = {"for_partner": 10000000000, "first_terms": 10000000000, "second_terms": 1000000000, "all_terms": 1000000000}
LIMIT = 32 * 1024 * 1024
ANY = pl.BlockSpec(memory_space=pl.ANY)


def params(limit=LIMIT):
    return pltpu.CompilerParams(vmem_limit_bytes=limit)


def column(place_ref, x, core):
    return pl.ds(pl.multiple_of((2 * x + core) * LANES, LANES), LANES)


def for_partner(place, grad, start, halves):
    def kernel(place_ref, grad_ref, *rest):
        sems = rest[-1]
        copies = []
        at = start
        for chunk, half in enumerate(halves):
            for x in range(4):
                copies.append(
                    pltpu.make_async_copy(
                        grad_ref.at[pl.ds(at, 2 * half), column(place_ref, x, 1 - place_ref[1])],
                        rest[chunk].at[x],
                        sems.at[chunk, x],
                    )
                )
            at += 2 * half
        for copy in copies:
            copy.start()
        for copy in copies:
            copy.wait()

    return pl.pallas_call(
        kernel,
        out_shape=[jax.ShapeDtypeStruct((4, 2 * half, LANES), BF16) for half in halves],
        in_specs=[pl.BlockSpec(memory_space=pltpu.SMEM), ANY],
        out_specs=[ANY] * len(halves),
        scratch_shapes=[pltpu.SemaphoreType.DMA((len(halves), 4))],
        compiler_params=params(),
        cost_estimate=pl.CostEstimate(flops=FLOPS["for_partner"], bytes_accessed=1000, transcendentals=0),
        name="for_partner",
    )(place, grad)


def whole(shape):
    return pl.BlockSpec(shape, lambda i: (0,) * len(shape))


def add_up(name, place, arrays, terms, outs, in_place=True, before=None):
    most = max(term[0] for term in terms)
    n_arrays = len(arrays)

    def kernel(place_ref, *rest):
        refs = rest[:n_arrays]
        rest = rest[n_arrays + (before is not None) :]
        out_refs = rest[: len(outs)]
        held, in_sems = rest[len(outs) : len(outs) + 2]
        coming, going = [], []
        for t, (rows, sources, (out, at)) in enumerate(terms):
            part = pl.ds(0, rows)
            index = sources[0][1]
            coming.append(
                pltpu.make_async_copy(refs[0].at[index(place_ref)], held.at[t, part], in_sems.at[t])
            )
            coming[-1].start()
            if not in_place:
                total, out_sems = rest[len(outs) + 2 :]
                going.append(pltpu.make_async_copy(total.at[t, part], out_refs[out].at[at], out_sems.at[t]))
        for t, (rows, sources, (out, at)) in enumerate(terms):
            coming[t].wait()
            value = held[t, pl.ds(0, rows)].astype(F32)
            for array, index in sources[1:]:
                value = value + refs[array][index(place_ref)].astype(F32)
            if in_place:
                out_refs[out][at] = value.astype(BF16)
            else:
                total[t, pl.ds(0, rows)] = value.astype(BF16)
                going[t].start()
        for copy in going:
            copy.wait()

    operands = (place, *arrays) + (() if before is None else (before,))
    scratch = [pltpu.VMEM((len(terms), most, LANES), BF16), pltpu.SemaphoreType.DMA((len(terms),))]
    return pl.pallas_call(
        kernel,
        grid=(1,),
        out_shape=[jax.ShapeDtypeStruct(out, BF16) for out in outs],
        in_specs=[pl.BlockSpec(memory_space=pltpu.SMEM), ANY]
        + [whole(array.shape) for array in arrays[1:]]
        + [ANY] * (before is not None),
        out_specs=[whole(out) if in_place else ANY for out in outs],
        scratch_shapes=scratch * (1 if in_place else 2),
        input_output_aliases={} if before is None else {len(operands) - 1: 0},
        compiler_params=params(),
        cost_estimate=pl.CostEstimate(flops=FLOPS[name], bytes_accessed=1000, transcendentals=0),
        name=name,
    )(*operands)


def own(start, half, h, mask):
    rows = pl.ds(start + h * half, half)
    return (0, lambda place_ref: (rows, column(place_ref, place_ref[0] ^ mask, place_ref[1])))


def partner(array, half, h, mask):
    rows = pl.ds(h * half, half)
    return (array, lambda place_ref: (place_ref[0] ^ mask, rows))


def first_terms(place, grad, near, start, half):
    terms = [
        (half, [own(start, half, h, mask), partner(1, half, h, mask)], (h, (j,)))
        for h in (0, 1)
        for j, mask in enumerate((1 + 2 * h, 2))
    ]
    return add_up("first_terms", place, (grad, near), terms, [(2, half, LANES)] * 2)


def second_terms(place, grad, near, got, start, half):
    terms = [
        (half, [own(start, half, h, 3 - 2 * h), partner(1, half, h, 3 - 2 * h), (2 + h, lambda _: (1,))], (h, (slice(None),)))
        for h in (0, 1)
    ]
    return add_up("second_terms", place, (grad, near, *got), terms, [(half, LANES)] * 2)


def all_terms(place, grad, chunks, before):
    arrays, terms = [grad], []
    for start, half, near, got, last in chunks:
        base = len(arrays)
        arrays += [near, *got, *last]
        for h in (0, 1):
            sources = [
                own(start, half, h, 0),
                partner(base, half, h, 0),
                (base + 1 + h, lambda _: (0,)),
                (base + 3 + h, lambda _: (slice(None),)),
            ]
            terms.append((half, sources, (0, (pl.ds(start + h * half, half),))))
    return add_up("all_terms", place, arrays, terms, [(grad.shape[0], LANES)], False, before)[0]


def adam(gradient, master, moment_one, moment_two):
    correct_one = 1.0 - beta_one**STEP
    correct_two = 1.0 - beta_two**STEP
    one = beta_one * moment_one + (1.0 - beta_one) * gradient
    two = beta_two * moment_two + (1.0 - beta_two) * gradient * gradient
    scaled = two * (1.0 / correct_two)
    update = one / (scaled * lax.rsqrt(scaled) + adam_eps)
    return (1.0 - learn_rate * decay_rate) * master - (learn_rate / correct_one) * update, one, two


GROUP = 8
STATE_GROUP = 4


def replica_terms(rows, owner_slot, slot_expert, master, moment_one, moment_two):
    experts, height, lanes = master.shape
    hosts, slots = slot_expert.shape

    def kernel(owner_ref, slot_ref, rows_ref, master_ref, one_ref, two_ref, out_ref, updated):
        step = pl.program_id(0)
        for k in range(GROUP):
            e = step * GROUP + k
            gradient = rows_ref[owner_ref[e]].astype(F32)
            updated[e] = adam(gradient, master_ref[k], one_ref[k], two_ref[k])[0].astype(BF16)

        @pl.when(step == experts // GROUP - 1)
        def _():
            for g in range(hosts):
                for s in range(slots):
                    out_ref[g, s] = updated[slot_ref[g, s]]

    state = pl.BlockSpec((GROUP, height, lanes), lambda i, *_: (i, 0, 0))
    return pl.pallas_call(
        kernel,
        out_shape=pltpu.HBM((hosts, slots, height, lanes), BF16),
        grid_spec=pltpu.PrefetchScalarGridSpec(
            num_scalar_prefetch=2,
            grid=(experts // GROUP,),
            in_specs=[pl.BlockSpec(rows.shape, lambda i, *_: (0, 0, 0)), state, state, state],
            out_specs=pl.BlockSpec((hosts, slots, height, lanes), lambda i, *_: (0, 0, 0, 0)),
            scratch_shapes=[pltpu.VMEM((experts, height, lanes), BF16)],
        ),
        compiler_params=params(50 * 1024 * 1024),
        name="replica_terms",
    )(owner_slot, slot_expert, rows, master, moment_one, moment_two)


def new_state(rows, owner_slot, master, moment_one, moment_two, ema_weights):
    experts, height, lanes = master.shape

    def kernel(owner_ref, rows_ref, master_ref, one_ref, two_ref, ema_ref, master_out, one_out, two_out, ema_out):
        for k in range(STATE_GROUP):
            gradient = rows_ref[owner_ref[pl.program_id(0) * STATE_GROUP + k]].astype(F32)
            weights, one, two = adam(gradient, master_ref[k], one_ref[k], two_ref[k])
            master_out[k] = weights
            one_out[k] = one
            two_out[k] = two
            ema_out[k] = ema_decay * ema_ref[k] + (1.0 - ema_decay) * weights

    state = pl.BlockSpec((STATE_GROUP, height, lanes), lambda i, *_: (i, 0, 0))
    return pl.pallas_call(
        kernel,
        out_shape=[jax.ShapeDtypeStruct(master.shape, F32)] * 4,
        grid_spec=pltpu.PrefetchScalarGridSpec(
            num_scalar_prefetch=1,
            grid=(experts // STATE_GROUP,),
            in_specs=[pl.BlockSpec(rows.shape, lambda i, *_: (0, 0, 0)), state, state, state, state],
            out_specs=[state] * 4,
        ),
        compiler_params=params(48 * 1024 * 1024),
        name="new_state",
    )(owner_slot, rows, master, moment_one, moment_two, ema_weights)


def by_slot(blocks):
    sources, slots, height, lanes = blocks.shape

    def kernel(in_ref, out_ref, sems):
        copies = [pltpu.make_async_copy(in_ref.at[:, s], out_ref.at[s], sems.at[s]) for s in range(slots)]
        for copy in copies:
            copy.start()
        for copy in copies:
            copy.wait()

    return pl.pallas_call(
        kernel,
        out_shape=jax.ShapeDtypeStruct((slots, sources, height, lanes), BF16),
        in_specs=[pl.BlockSpec(memory_space=pl.ANY)],
        out_specs=pl.BlockSpec(memory_space=pl.ANY),
        scratch_shapes=[pltpu.SemaphoreType.DMA((slots,))],
        compiler_params=params(),
        name="by_slot",
    )(blocks)


def exchange(value, mask):
    return lax.ppermute(value, "dp", [(i, i ^ mask) for i in range(8)])


def after(value, other):
    return lax.optimization_barrier((value, other))[0]


def per_device(grad_parts, owner_slot, slot_expert, master, moment_one, moment_two, ema_weights):
    grad = grad_parts[0, 0]
    total_rows = grad.shape[0]
    experts, height, _ = master.shape
    me = lax.axis_index("dp").astype(jnp.int32)
    place = jnp.stack([me // 2, me % 2])

    starts = [2 * sum(CHUNKS[:k]) for k in range(len(CHUNKS))]
    first = for_partner(place, grad, 0, CHUNKS[:1])
    later = for_partner(after(place, first[0]), grad, starts[1], CHUNKS[1:])
    nears = [exchange(block, 1) for block in (*first, *later)]
    gots, lasts = [], []
    for start, half, near in zip(starts, CHUNKS, nears):
        a, b = first_terms(place, grad, near, start, half)
        gots.append((exchange(a, 2), exchange(b, 6)))
        place = after(place, a)
    for start, half, near, got in zip(starts, CHUNKS, nears, gots):
        a, b = second_terms(place, grad, near, got, start, half)
        lasts.append((exchange(a, 6), exchange(b, 2)))
        place = after(place, a)
    chunks = list(zip(starts, CHUNKS, nears, gots, lasts))
    summed = None
    for k in range(len(chunks)):
        summed = all_terms(place, grad, chunks[k : k + 1], summed)

    rows = lax.all_to_all(
        summed.reshape(experts, height, LANES), "expert", split_axis=0, concat_axis=0, tiled=True
    )
    to_hosts = replica_terms(rows, owner_slot, slot_expert, master, moment_one, moment_two)
    state = new_state(rows, owner_slot, master, moment_one, moment_two, ema_weights)
    replicas = lax.all_to_all(to_hosts, "expert", split_axis=0, concat_axis=0, tiled=True)
    replicas = by_slot(replicas).reshape(-1, total_rows, LANES)
    return (*state, replicas)


def solution(mesh):
    placed = (
        P("dp", "expert", None, None),
        P(),
        P(),
        P(None, "expert", "dp"),
        P(None, "expert", "dp"),
        P(None, "expert", "dp"),
        P(None, "expert", "dp"),
    )
    return jax.shard_map(
        per_device,
        mesh=mesh,
        in_specs=placed,
        out_specs=(
            P(None, "expert", "dp"),
            P(None, "expert", "dp"),
            P(None, "expert", "dp"),
            P(None, "expert", "dp"),
            P("expert", None, "dp"),
        ),
        check_vma=False,
    )
```

```python
import jax
import jax.numpy as jnp
from jax import lax
from jax.experimental import pallas as pl
from jax.experimental.pallas import tpu as pltpu
from jax.sharding import PartitionSpec as P

STEP = 10

beta_one = 0.9
beta_two = 0.999
adam_eps = 1e-08
learn_rate = 0.05
decay_rate = 0.1
ema_decay = 0.99

F32 = jnp.float32
BF16 = jnp.bfloat16
LANES = 128
CHUNKS = (448, 800, 544)
FLOPS = {"for_partner": 10000000000, "first_terms": 10000000000, "second_terms": 1000000000, "all_terms": 1000000000}
LIMIT = 32 * 1024 * 1024
ANY = pl.BlockSpec(memory_space=pl.ANY)


def params(limit=LIMIT):
    return pltpu.CompilerParams(vmem_limit_bytes=limit)


def column(place_ref, x, core):
    return pl.ds(pl.multiple_of((2 * x + core) * LANES, LANES), LANES)


def for_partner(place, grad, start, halves):
    def kernel(place_ref, grad_ref, *rest):
        sems = rest[-1]
        copies = []
        at = start
        for chunk, half in enumerate(halves):
            for x in range(4):
                copies.append(
                    pltpu.make_async_copy(
                        grad_ref.at[pl.ds(at, 2 * half), column(place_ref, x, 1 - place_ref[1])],
                        rest[chunk].at[x],
                        sems.at[chunk, x],
                    )
                )
            at += 2 * half
        for copy in copies:
            copy.start()
        for copy in copies:
            copy.wait()

    return pl.pallas_call(
        kernel,
        out_shape=[jax.ShapeDtypeStruct((4, 2 * half, LANES), BF16) for half in halves],
        in_specs=[pl.BlockSpec(memory_space=pltpu.SMEM), ANY],
        out_specs=[ANY] * len(halves),
        scratch_shapes=[pltpu.SemaphoreType.DMA((len(halves), 4))],
        compiler_params=params(),
        cost_estimate=pl.CostEstimate(flops=FLOPS["for_partner"], bytes_accessed=1000, transcendentals=0),
        name="for_partner",
    )(place, grad)


def whole(shape):
    return pl.BlockSpec(shape, lambda i: (0,) * len(shape))


def add_up(name, place, arrays, terms, outs, in_place=True, before=None):
    most = max(term[0] for term in terms)
    n_arrays = len(arrays)

    def kernel(place_ref, *rest):
        refs = rest[:n_arrays]
        rest = rest[n_arrays + (before is not None) :]
        out_refs = rest[: len(outs)]
        held, in_sems = rest[len(outs) : len(outs) + 2]
        coming, going = [], []
        for t, (rows, sources, (out, at)) in enumerate(terms):
            part = pl.ds(0, rows)
            index = sources[0][1]
            coming.append(
                pltpu.make_async_copy(refs[0].at[index(place_ref)], held.at[t, part], in_sems.at[t])
            )
            coming[-1].start()
            if not in_place:
                total, out_sems = rest[len(outs) + 2 :]
                going.append(pltpu.make_async_copy(total.at[t, part], out_refs[out].at[at], out_sems.at[t]))
        for t, (rows, sources, (out, at)) in enumerate(terms):
            coming[t].wait()
            value = held[t, pl.ds(0, rows)].astype(F32)
            for array, index in sources[1:]:
                value = value + refs[array][index(place_ref)].astype(F32)
            if in_place:
                out_refs[out][at] = value.astype(BF16)
            else:
                total[t, pl.ds(0, rows)] = value.astype(BF16)
                going[t].start()
        for copy in going:
            copy.wait()

    operands = (place, *arrays) + (() if before is None else (before,))
    scratch = [pltpu.VMEM((len(terms), most, LANES), BF16), pltpu.SemaphoreType.DMA((len(terms),))]
    return pl.pallas_call(
        kernel,
        grid=(1,),
        out_shape=[jax.ShapeDtypeStruct(out, BF16) for out in outs],
        in_specs=[pl.BlockSpec(memory_space=pltpu.SMEM), ANY]
        + [whole(array.shape) for array in arrays[1:]]
        + [ANY] * (before is not None),
        out_specs=[whole(out) if in_place else ANY for out in outs],
        scratch_shapes=scratch * (1 if in_place else 2),
        input_output_aliases={} if before is None else {len(operands) - 1: 0},
        compiler_params=params(),
        cost_estimate=pl.CostEstimate(flops=FLOPS[name], bytes_accessed=1000, transcendentals=0),
        name=name,
    )(*operands)


def own(start, half, h, mask):
    rows = pl.ds(start + h * half, half)
    return (0, lambda place_ref: (rows, column(place_ref, place_ref[0] ^ mask, place_ref[1])))


def partner(array, half, h, mask):
    rows = pl.ds(h * half, half)
    return (array, lambda place_ref: (place_ref[0] ^ mask, rows))


def first_terms(place, grad, near, start, half):
    terms = [
        (half, [own(start, half, h, mask), partner(1, half, h, mask)], (h, (j,)))
        for h in (0, 1)
        for j, mask in enumerate((1 + 2 * h, 2))
    ]
    return add_up("first_terms", place, (grad, near), terms, [(2, half, LANES)] * 2)


def second_terms(place, grad, near, got, start, half):
    terms = [
        (half, [own(start, half, h, 3 - 2 * h), partner(1, half, h, 3 - 2 * h), (2 + h, lambda _: (1,))], (h, (slice(None),)))
        for h in (0, 1)
    ]
    return add_up("second_terms", place, (grad, near, *got), terms, [(half, LANES)] * 2)


def all_terms(place, grad, chunks, before):
    arrays, terms = [grad], []
    for start, half, near, got, last in chunks:
        base = len(arrays)
        arrays += [near, *got, *last]
        for h in (0, 1):
            sources = [
                own(start, half, h, 0),
                partner(base, half, h, 0),
                (base + 1 + h, lambda _: (0,)),
                (base + 3 + h, lambda _: (slice(None),)),
            ]
            terms.append((half, sources, (0, (pl.ds(start + h * half, half),))))
    return add_up("all_terms", place, arrays, terms, [(grad.shape[0], LANES)], False, before)[0]


def adam(gradient, master, moment_one, moment_two):
    correct_one = 1.0 - beta_one**STEP
    correct_two = 1.0 - beta_two**STEP
    one = beta_one * moment_one + (1.0 - beta_one) * gradient
    two = beta_two * moment_two + (1.0 - beta_two) * gradient * gradient
    scaled = two * (1.0 / correct_two)
    update = one / (scaled * lax.rsqrt(scaled) + adam_eps)
    return (1.0 - learn_rate * decay_rate) * master - (learn_rate / correct_one) * update, one, two


GROUP = 8
STATE_GROUP = 4


def replica_terms(rows, owner_slot, slot_expert, master, moment_one, moment_two):
    experts, height, lanes = master.shape
    hosts, slots = slot_expert.shape

    def kernel(owner_ref, slot_ref, rows_ref, master_ref, one_ref, two_ref, out_ref, updated, packed, out_sems):
        step = pl.program_id(0)
        for k in range(GROUP):
            e = step * GROUP + k
            gradient = rows_ref[owner_ref[e]].astype(F32)
            updated[e] = adam(gradient, master_ref[k], one_ref[k], two_ref[k])[0].astype(BF16)

        @pl.when(step == experts // GROUP - 1)
        def _():
            copies = []
            for g in range(hosts):
                for s in range(slots):
                    packed[g, s] = updated[slot_ref[g, s]]
                copies.append(pltpu.make_async_copy(packed.at[g], out_ref.at[g], out_sems.at[g]))
                copies[-1].start()
            for copy in copies:
                copy.wait()

    state = pl.BlockSpec((GROUP, height, lanes), lambda i, *_: (i, 0, 0))
    return pl.pallas_call(
        kernel,
        out_shape=pltpu.HBM((hosts, slots, height, lanes), BF16),
        grid_spec=pltpu.PrefetchScalarGridSpec(
            num_scalar_prefetch=2,
            grid=(experts // GROUP,),
            in_specs=[pl.BlockSpec(rows.shape, lambda i, *_: (0, 0, 0)), state, state, state],
            out_specs=pl.BlockSpec(memory_space=pltpu.HBM),
            scratch_shapes=[
                pltpu.VMEM((experts, height, lanes), BF16),
                pltpu.VMEM((hosts, slots, height, lanes), BF16),
                pltpu.SemaphoreType.DMA((hosts,)),
            ],
        ),
        compiler_params=params(50 * 1024 * 1024),
        name="replica_terms",
    )(owner_slot, slot_expert, rows, master, moment_one, moment_two)


def new_state(rows, owner_slot, master, moment_one, moment_two, ema_weights):
    experts, height, lanes = master.shape

    def kernel(owner_ref, rows_ref, master_ref, one_ref, two_ref, ema_ref, master_out, one_out, two_out, ema_out):
        for k in range(STATE_GROUP):
            gradient = rows_ref[owner_ref[pl.program_id(0) * STATE_GROUP + k]].astype(F32)
            weights, one, two = adam(gradient, master_ref[k], one_ref[k], two_ref[k])
            master_out[k] = weights
            one_out[k] = one
            two_out[k] = two
            ema_out[k] = ema_decay * ema_ref[k] + (1.0 - ema_decay) * weights

    state = pl.BlockSpec((STATE_GROUP, height, lanes), lambda i, *_: (i, 0, 0))
    return pl.pallas_call(
        kernel,
        out_shape=[jax.ShapeDtypeStruct(master.shape, F32)] * 4,
        grid_spec=pltpu.PrefetchScalarGridSpec(
            num_scalar_prefetch=1,
            grid=(experts // STATE_GROUP,),
            in_specs=[pl.BlockSpec(rows.shape, lambda i, *_: (0, 0, 0)), state, state, state, state],
            out_specs=[state] * 4,
        ),
        compiler_params=params(48 * 1024 * 1024),
        name="new_state",
    )(owner_slot, rows, master, moment_one, moment_two, ema_weights)


def by_slot(blocks):
    sources, slots, height, lanes = blocks.shape

    def kernel(in_ref, out_ref, sems):
        copies = [pltpu.make_async_copy(in_ref.at[:, s], out_ref.at[s], sems.at[s]) for s in range(slots)]
        for copy in copies:
            copy.start()
        for copy in copies:
            copy.wait()

    return pl.pallas_call(
        kernel,
        out_shape=jax.ShapeDtypeStruct((slots, sources, height, lanes), BF16),
        in_specs=[pl.BlockSpec(memory_space=pl.ANY)],
        out_specs=pl.BlockSpec(memory_space=pl.ANY),
        scratch_shapes=[pltpu.SemaphoreType.DMA((slots,))],
        compiler_params=params(),
        name="by_slot",
    )(blocks)


def exchange(value, mask):
    return lax.ppermute(value, "dp", [(i, i ^ mask) for i in range(8)])


def after(value, other):
    return lax.optimization_barrier((value, other))[0]


def per_device(grad_parts, owner_slot, slot_expert, master, moment_one, moment_two, ema_weights):
    grad = grad_parts[0, 0]
    total_rows = grad.shape[0]
    experts, height, _ = master.shape
    me = lax.axis_index("dp").astype(jnp.int32)
    place = jnp.stack([me // 2, me % 2])

    starts = [2 * sum(CHUNKS[:k]) for k in range(len(CHUNKS))]
    first = for_partner(place, grad, 0, CHUNKS[:1])
    later = for_partner(after(place, first[0]), grad, starts[1], CHUNKS[1:])
    nears = [exchange(block, 1) for block in (*first, *later)]
    gots, lasts = [], []
    for start, half, near in zip(starts, CHUNKS, nears):
        a, b = first_terms(place, grad, near, start, half)
        gots.append((exchange(a, 2), exchange(b, 6)))
        place = after(place, a)
    for start, half, near, got in zip(starts, CHUNKS, nears, gots):
        a, b = second_terms(place, grad, near, got, start, half)
        lasts.append((exchange(a, 6), exchange(b, 2)))
        place = after(place, a)
    chunks = list(zip(starts, CHUNKS, nears, gots, lasts))
    summed = None
    for k in range(len(chunks)):
        summed = all_terms(place, grad, chunks[k : k + 1], summed)

    rows = lax.all_to_all(
        summed.reshape(experts, height, LANES), "expert", split_axis=0, concat_axis=0, tiled=True
    )
    to_hosts = replica_terms(rows, owner_slot, slot_expert, master, moment_one, moment_two)
    state = new_state(rows, owner_slot, master, moment_one, moment_two, ema_weights)
    replicas = lax.all_to_all(to_hosts, "expert", split_axis=0, concat_axis=0, tiled=True)
    replicas = by_slot(replicas).reshape(-1, total_rows, LANES)
    return (*state, replicas)


def solution(mesh):
    placed = (
        P("dp", "expert", None, None),
        P(),
        P(),
        P(None, "expert", "dp"),
        P(None, "expert", "dp"),
        P(None, "expert", "dp"),
        P(None, "expert", "dp"),
    )
    return jax.shard_map(
        per_device,
        mesh=mesh,
        in_specs=placed,
        out_specs=(
            P(None, "expert", "dp"),
            P(None, "expert", "dp"),
            P(None, "expert", "dp"),
            P(None, "expert", "dp"),
            P("expert", None, "dp"),
        ),
        check_vma=False,
    )
```
